512 devices in a mesh: dp: 32 (over y, x), tensor: 16 (over z, core).
Axes of the slice: x: 4, y: 8, z: 8, core: 2. Of those that a mesh axis runs over, the one named last changes fastest.
Arguments:
- gate_pre: bfloat16 [8192, 28672], P('dp', 'tensor'), parts along dimension 0, may hold values from -6 to 6
- up_pre: bfloat16 [8192, 28672], P('dp', 'tensor'), parts along dimension 0, may hold values from -6 to 6
- signs: int32 [28672], P('tensor'), may hold values from -1 to 1, as said below
- hadamard: int32 [28, 28], replicated, may hold values from -1 to 1, as said below
- down_weight: bfloat16 [28672, 4096], P('tensor'), may hold values from -0.03125 to 0.03125
Outputs:
- mixed: bfloat16 [8192, 4096], P(('dp', 'tensor')), parts along dimension 0
The draws below stay inside these ranges and needn't reach their ends.
There are 32 independent parts, one for each index of `dp`. The reference program is written for one: setup_inputs(seed, part) draws one part's arguments, and reference() takes and returns one part's arrays. A program takes and returns all parts, laid end to end along the dimension named above; an argument that names none is the same for every part. Nothing has to cross between parts.
Inputs may be any that keep to these rules, and one draw needn't show every extreme that they name: `signs`: every entry is -1 or 1. `hadamard`: a Hadamard matrix: entries -1 or 1, any two distinct rows orthogonal.
All inputs are finite; a program needn't handle non-finite values.
Results may differ from the reference program's by a relative error of at most 0.028.
Values may be sent and summed in bfloat16 or wider, within the bound.
No kernel may reach another device: no remote copies, remote signals or barrier semaphores. Data moves between devices by JAX's collectives and lax.ppermute only.
A program may use at most 64 MiB of HBM per device.

```python
import math
import jax
import jax.numpy as jnp
import numpy as np
from jax import lax

TOKENS = 256
FFN_UNITS = 28672
OUT_WIDTH = 4096
SYLVESTER = 1024
N_TENSOR = 16


def paley_matrix():
    squares = set((value * value % 13 for value in range(1, 13)))
    conference = np.zeros((14, 14), dtype=np.int64)
    for column in range(1, 14):
        conference[0, column] = 1
        conference[column, 0] = 1
    for row in range(13):
        for column in range(13):
            offset = (row - column) % 13
            if offset != 0:
                conference[row + 1, column + 1] = 1 if offset in squares else -1
    upper = np.array([[1, 1], [1, -1]], dtype=np.int64)
    lower = np.array([[1, -1], [-1, -1]], dtype=np.int64)
    return np.kron(conference, upper) + np.kron(np.eye(14, dtype=np.int64), lower)


def draw_signs(key, part):
    key = jax.random.fold_in(key, 1)
    flips = jax.random.randint(key, (FFN_UNITS,), 0, 2, dtype=jnp.int32)
    return (2 * flips - 1).astype(jnp.int32)


def draw_hadamard(key, part):
    key = jax.random.fold_in(key, 2)
    keys = jax.random.split(key, 4)
    base = jnp.asarray(paley_matrix(), dtype=jnp.int32)
    row_order = jax.random.permutation(keys[0], 28)
    column_order = jax.random.permutation(keys[1], 28)
    row_signs = 2 * jax.random.randint(keys[2], (28,), 0, 2, dtype=jnp.int32) - 1
    column_signs = 2 * jax.random.randint(keys[3], (28,), 0, 2, dtype=jnp.int32) - 1
    shuffled = base[row_order][:, column_order]
    return (shuffled * row_signs[:, None] * column_signs[None, :]).astype(jnp.int32)


def steps_of(own_key, extent, pieces, low, largest):
    loudness = 1.0
    for dim, blocks in pieces:
        steps = jax.random.uniform(jax.random.fold_in(jax.random.fold_in(own_key, 6), dim), (blocks,), jnp.float32, low / len(pieces), largest / len(pieces))
        loudness = loudness * jnp.repeat(jnp.exp(steps), extent[dim] // blocks).reshape((-1,) + (1,) * (len(extent) - 1 - dim))
    return loudness


def normal_values(stream_key, dims, spread, reach, pieces=(), kind=jnp.bfloat16):
    factor_of = steps_of(stream_key, dims, pieces, -0.22, 0.18) if pieces else 1.0
    drawn = jax.random.normal(stream_key, dims, jnp.float32) * spread * factor_of
    return jnp.minimum(jnp.maximum(drawn, -reach), reach).astype(kind)


def setup_inputs(seed: int = 0, part: int = 0) -> dict:
    key_list = jax.random.split(jax.random.key(seed), 6)
    part_keys = jax.random.split(jax.random.fold_in(key_list[5], part), 6)
    return {
        "gate_pre": normal_values(part_keys[0], (TOKENS, FFN_UNITS), 1.0, 6.0, ((1, 16),)),
        "up_pre": normal_values(part_keys[1], (TOKENS, FFN_UNITS), 1.0, 6.0, ((1, 16),)),
        "signs": draw_signs(jax.random.fold_in(key_list[5], 71), part),
        "hadamard": draw_hadamard(jax.random.fold_in(key_list[5], 71), part),
        "down_weight": normal_values(key_list[4], (FFN_UNITS, OUT_WIDTH), FFN_UNITS ** -0.5, 0.03125, ((0, 16),)),
    }


def sylvester_matrix(order):
    position = jnp.arange(order, dtype=jnp.int32)
    common = position[:, None] & position[None, :]
    parity = jnp.zeros((order, order), dtype=jnp.int32)
    for bit_index in range(max(order.bit_length(), 1)):
        parity = parity + (common >> bit_index & 1)
    parity = parity % 2
    return (1 - 2 * parity).astype(jnp.float32)

def reference(gate_pre, up_pre, signs, hadamard, down_weight):
    hidden = jax.nn.silu(gate_pre.astype(jnp.float32)) * up_pre.astype(jnp.float32) * signs.astype(jnp.float32)[None, :]
    blocks = hidden.reshape(TOKENS, SYLVESTER, 28)
    inner = jnp.einsum('tba,ae->tbe', blocks, hadamard.astype(jnp.float32), precision=lax.Precision.HIGHEST)
    outer = jnp.einsum('tbe,bc->tce', inner, sylvester_matrix(SYLVESTER), precision=lax.Precision.HIGHEST)
    rotated = (outer.reshape(TOKENS, FFN_UNITS) / math.sqrt(FFN_UNITS)).astype(jnp.bfloat16)
    group = FFN_UNITS // N_TENSOR
    total = jnp.zeros((TOKENS, OUT_WIDTH), dtype=jnp.float32)
    for index in range(N_TENSOR):
        piece = jnp.dot(rotated[:, index * group:(index + 1) * group], down_weight[index * group:(index + 1) * group, :], preferred_element_type=jnp.float32)
        total = total + piece.astype(jnp.bfloat16).astype(jnp.float32)
    return total.astype(jnp.bfloat16)
```

```python
import math

import jax
import jax.numpy as jnp
import numpy as np
from jax import lax
from jax.experimental import pallas as pl
from jax.experimental.pallas import tpu as pltpu
from jax.sharding import PartitionSpec as P

FFN_UNITS = 28672
ORDER = 28
INNER = 32
SLAB = ORDER * INNER
LANES = 128


def sylvester(order):
    index = np.arange(order)
    common = index[:, None] & index[None, :]
    parity = np.zeros((order, order), np.int64)
    for bit in range(order.bit_length()):
        parity += common >> bit & 1
    return 1 - 2 * (parity % 2)


def slab_patterns():
    unit = np.arange(SLAB)
    outer = sylvester(INNER)[unit[:, None] // ORDER, unit[None, :] // ORDER]
    pick = (np.arange(INNER)[:, None] == unit[None, :] % ORDER)
    return outer, pick


def local_kernel(gate, up, signs, hadamard, outer, pick, pick_t, out, matrix):
    @pl.when(pl.program_id(0) == 0)
    def _():
        rows = jnp.dot(pick_t[...], hadamard[...], preferred_element_type=jnp.float32)
        spread = jnp.dot(
            rows.astype(jnp.bfloat16), pick[...], preferred_element_type=jnp.float32
        )
        matrix[...] = (spread * outer[...].astype(jnp.float32)).astype(jnp.bfloat16)

    half = 0.5 * gate[...].astype(jnp.float32)
    hidden = (half + half * jnp.tanh(half)) * (
        up[...].astype(jnp.float32) * signs[...].astype(jnp.float32)
    )
    out[...] = jnp.dot(
        hidden.astype(jnp.bfloat16), matrix[...], preferred_element_type=jnp.float32
    ).astype(jnp.bfloat16)


def local_transform(gate, up, signs, hadamard):
    tokens, width = gate.shape
    outer, pick = slab_patterns()
    padded = jnp.zeros((INNER, INNER), jnp.bfloat16).at[:ORDER, :ORDER].set(
        hadamard.astype(jnp.bfloat16)
    )
    whole = lambda shape: pl.BlockSpec(shape, lambda i: (0, 0))
    piece = pl.BlockSpec((tokens, SLAB), lambda i: (0, i))
    return pl.pallas_call(
        local_kernel,
        grid=(width // SLAB,),
        in_specs=[
            piece,
            piece,
            pl.BlockSpec((1, SLAB), lambda i: (0, i)),
            whole((INNER, INNER)),
            whole((SLAB, SLAB)),
            whole((INNER, SLAB)),
            whole((SLAB, INNER)),
        ],
        out_specs=piece,
        out_shape=jax.ShapeDtypeStruct((tokens, width), jnp.bfloat16),
        scratch_shapes=[pltpu.VMEM((SLAB, SLAB), jnp.bfloat16)],
        compiler_params=pltpu.CompilerParams(vmem_limit_bytes=24 << 20),
        name="local_transform",
    )(
        gate,
        up,
        signs.reshape(1, width),
        padded,
        jnp.asarray(outer, jnp.bfloat16),
        jnp.asarray(pick, jnp.bfloat16),
        jnp.asarray(pick.T, jnp.bfloat16),
    )


def across_kernel(scale, source, out):
    devices, tokens, width = source.shape
    slabs = width // SLAB
    for chunk in range(SLAB // LANES):
        values = []
        for device in range(devices):
            for slab in range(slabs):
                lanes = pl.ds(slab * SLAB + chunk * LANES, LANES)
                values.append(source[device, :, lanes].astype(jnp.float32))
        step = 1
        while step < len(values):
            for low in range(len(values)):
                if low & step == 0:
                    a, b = values[low], values[low | step]
                    values[low], values[low | step] = a + b, a - b
            step *= 2
        for index, value in enumerate(values):
            device, slab = divmod(index, slabs)
            lanes = pl.ds(slab * SLAB + chunk * LANES, LANES)
            out[device, :, lanes] = (value * scale).astype(jnp.bfloat16)


def across_transform(source):
    return pl.pallas_call(
        lambda source, out: across_kernel(1.0 / math.sqrt(FFN_UNITS), source, out),
        in_specs=[pl.BlockSpec(memory_space=pltpu.VMEM)],
        out_specs=pl.BlockSpec(memory_space=pltpu.VMEM),
        out_shape=jax.ShapeDtypeStruct(source.shape, jnp.bfloat16),
        compiler_params=pltpu.CompilerParams(vmem_limit_bytes=24 << 20),
        name="across_transform",
    )(source)


def per_device(gate_pre, up_pre, signs, hadamard, down_weight):
    parts = lax.axis_size("tensor")
    tokens, width = gate_pre.shape
    own = tokens // parts
    chips = parts // 2
    core = lax.axis_index("tensor") % 2
    inner = local_transform(gate_pre, up_pre, signs, hadamard)
    gathered = lax.all_to_all(inner.reshape(parts, own, width), "tensor", 0, 0)
    rotated = across_transform(gathered)
    back = lax.all_to_all(rotated, "tensor", 0, 0).reshape(chips, 2, own, width)

    def product(which):
        rows = lax.dynamic_index_in_dim(back, which, 1, keepdims=False)
        return jnp.dot(
            rows.reshape(chips * own, width), down_weight, preferred_element_type=jnp.float32
        ).astype(jnp.bfloat16)

    pairs = [(source, source ^ 1) for source in range(parts)]
    other = lax.ppermute(product(1 - core), "tensor", pairs)
    mine = product(core)
    both = (mine.astype(jnp.float32) + other.astype(jnp.float32)).astype(jnp.bfloat16)
    same_core = [[2 * chip + side for chip in range(chips)] for side in range(2)]
    terms = lax.all_to_all(
        both.reshape(chips, own, -1), "tensor", 0, 0, axis_index_groups=same_core
    )
    return jnp.sum(terms.astype(jnp.float32), axis=0).astype(jnp.bfloat16)


def solution(mesh):
    placed = (P("dp", "tensor"), P("dp", "tensor"), P("tensor"), P(), P("tensor", None))
    return jax.shard_map(
        per_device, mesh=mesh, in_specs=placed, out_specs=P(("dp", "tensor"), None), check_vma=False
    )
```

```python
import math

import jax
import jax.numpy as jnp
from jax import lax
from jax.experimental import pallas as pl
from jax.experimental.pallas import tpu as pltpu
from jax.sharding import PartitionSpec as P

FFN_UNITS = 28672
ORDER = 28
INNER = 32
SLAB = ORDER * INNER
LANES = 128
COLUMNS = 512


def outer_index(unit):
    return (unit * 2341) >> 16


def iota(shape, dim):
    return lax.broadcasted_iota(jnp.int32, shape, dim)


def picks(condition):
    return jnp.where(condition, 1.0, 0.0).astype(jnp.bfloat16)


def slab_matrix(hadamard):
    tall, wide = (SLAB, INNER), (INNER, SLAB)
    tall_unit, wide_unit = iota(tall, 0), iota(wide, 1)
    tall_outer, wide_outer = outer_index(tall_unit), outer_index(wide_unit)
    pick_outer = picks(wide_outer == iota(wide, 0))
    pick_inner = picks(wide_unit - ORDER * wide_outer == iota(wide, 0))[:ORDER]
    tall_inner = picks(tall_unit - ORDER * tall_outer == iota(tall, 1))[:, :ORDER]
    common = tall_outer & iota(tall, 1)
    for shift in (4, 2, 1):
        common = common ^ (common >> shift)
    outer_rows = (1 - 2 * (common & 1)).astype(jnp.float32).astype(jnp.bfloat16)
    inner_rows = jnp.dot(
        tall_inner,
        hadamard.astype(jnp.float32).astype(jnp.bfloat16),
        preferred_element_type=jnp.float32,
    ).astype(jnp.bfloat16)
    inner = jnp.dot(inner_rows, pick_inner, preferred_element_type=jnp.float32)
    outer = jnp.dot(outer_rows, pick_outer, preferred_element_type=jnp.float32)
    return (inner * outer).astype(jnp.bfloat16)


def local_kernel(
    gate_hbm, up_hbm, signs_hbm, hadamard_hbm, out, gate, up, signs, hadamard, matrix, arrived, ready
):
    width = gate.shape[1]
    small = [
        pltpu.make_async_copy(source, held, ready.at[index])
        for index, (source, held) in enumerate(((hadamard_hbm, hadamard), (signs_hbm, signs)))
    ]
    for copy in small:
        copy.start()
    copies = []
    for slab in range(width // SLAB):
        lanes = pl.ds(slab * SLAB, SLAB)
        pair = [
            pltpu.make_async_copy(source.at[:, lanes], held.at[:, lanes], arrived.at[slab, index])
            for index, (source, held) in enumerate(((gate_hbm, gate), (up_hbm, up)))
        ]
        for copy in pair:
            copy.start()
        copies.append(pair)
    for copy in small:
        copy.wait()
    matrix[...] = slab_matrix(hadamard[...])
    for slab, pair in enumerate(copies):
        for copy in pair:
            copy.wait()
        lanes = pl.ds(slab * SLAB, SLAB)
        half = 0.5 * gate[:, lanes].astype(jnp.float32)
        sign = signs[lanes].astype(jnp.float32).reshape(1, SLAB)
        hidden = (half + half * jnp.tanh(half)) * (up[:, lanes].astype(jnp.float32) * sign)
        out[:, lanes] = jnp.dot(
            hidden.astype(jnp.bfloat16), matrix[...], preferred_element_type=jnp.float32
        ).astype(jnp.bfloat16)


def local_transform(gate, up, signs, hadamard):
    tokens, width = gate.shape
    vmem = pl.BlockSpec(memory_space=pltpu.VMEM)
    return pl.pallas_call(
        local_kernel,
        in_specs=[pl.BlockSpec(memory_space=pl.ANY)] * 4,
        out_specs=vmem,
        out_shape=jax.ShapeDtypeStruct((tokens, width), jnp.bfloat16),
        scratch_shapes=[
            pltpu.VMEM((tokens, width), jnp.bfloat16),
            pltpu.VMEM((tokens, width), jnp.bfloat16),
            pltpu.VMEM((width,), jnp.int32),
            pltpu.VMEM((ORDER, ORDER), jnp.int32),
            pltpu.VMEM((SLAB, SLAB), jnp.bfloat16),
            pltpu.SemaphoreType.DMA((width // SLAB, 2)),
            pltpu.SemaphoreType.DMA((2,)),
        ],
        compiler_params=pltpu.CompilerParams(vmem_limit_bytes=59 << 20),
        name="local_transform",
    )(gate, up, signs, hadamard)


def across_kernel(source, out):
    devices, tokens, width = source.shape
    slabs = width // SLAB
    core = lax.axis_index("tensor") % 2
    for chunk in range(SLAB // LANES):
        values = []
        for device in range(devices):
            for slab in range(slabs):
                lanes = pl.ds(slab * SLAB + chunk * LANES, LANES)
                values.append(source[device, :, lanes].astype(jnp.float32))
        step = 1
        while step < len(values):
            for low in range(len(values)):
                if low & step == 0:
                    a, b = values[low], values[low | step]
                    values[low], values[low | step] = a + b, a - b
            step *= 2
        for index, value in enumerate(values):
            device, slab = divmod(index, slabs)
            chip, side = divmod(device, 2)
            lanes = pl.ds(slab * SLAB + chunk * LANES, LANES)
            place = core if side == 0 else 1 - core
            out[chip, place, :, lanes] = (value * (1.0 / math.sqrt(FFN_UNITS))).astype(jnp.bfloat16)


def across_transform(source):
    devices, tokens, width = source.shape
    return pl.pallas_call(
        across_kernel,
        in_specs=[pl.BlockSpec(memory_space=pltpu.VMEM)],
        out_specs=pl.BlockSpec(memory_space=pltpu.VMEM),
        out_shape=jax.ShapeDtypeStruct((devices // 2, 2, tokens, width), jnp.bfloat16),
        compiler_params=pltpu.CompilerParams(vmem_limit_bytes=20 << 20),
        name="across_transform",
    )(source)


def product_kernel(rows, other, own_hbm, out, own, arrived):
    tiles = arrived.shape[0]
    chips, _, tokens, width = rows.shape
    lanes = lambda tile: pl.ds(pl.multiple_of(tile * COLUMNS, COLUMNS), COLUMNS)
    copy = lambda tile: pltpu.make_async_copy(
        own_hbm.at[:, lanes(tile)], own.at[:, lanes(tile)], arrived.at[tile]
    )
    for tile in range(tiles):
        copy(tile).start()

    @pl.loop(0, tiles)
    def _(tile):
        copy(tile).wait()
        total = other[:, lanes(tile)] + jnp.dot(
            rows[:, 0].reshape(chips * tokens, width),
            own[:, lanes(tile)],
            preferred_element_type=jnp.float32,
        )
        out[:, :, lanes(tile)] = total.astype(jnp.bfloat16).reshape(chips, tokens, COLUMNS)


def product(rows, other, own):
    chips, _, tokens, width = rows.shape
    columns = own.shape[1]
    vmem = pl.BlockSpec(memory_space=pltpu.VMEM)
    return pl.pallas_call(
        product_kernel,
        in_specs=[vmem, vmem, pl.BlockSpec(memory_space=pl.ANY)],
        out_specs=vmem,
        out_shape=jax.ShapeDtypeStruct((chips, tokens, columns), jnp.bfloat16),
        scratch_shapes=[
            pltpu.VMEM(own.shape, own.dtype),
            pltpu.SemaphoreType.DMA((columns // COLUMNS,)),
        ],
        compiler_params=pltpu.CompilerParams(vmem_limit_bytes=50 << 20),
        cost_estimate=pl.CostEstimate(
            flops=2 * chips * tokens * width * columns,
            transcendentals=0,
            bytes_accessed=own.size * own.dtype.itemsize,
        ),
        name="product",
    )(rows, other, own)


def per_device(gate_pre, up_pre, signs, hadamard, down_weight):
    parts = lax.axis_size("tensor")
    tokens, width = gate_pre.shape
    own = tokens // parts
    chips = parts // 2
    same_core = [[2 * chip + side for chip in range(chips)] for side in range(2)]
    pairs = [(source, source ^ 1) for source in range(parts)]
    inner = local_transform(gate_pre, up_pre, signs, hadamard)
    inner, down_weight = lax.optimization_barrier((inner, down_weight))
    other_weight = lax.ppermute(down_weight, "tensor", pairs)
    gathered = lax.all_to_all(inner.reshape(parts, own, width), "tensor", 0, 0)
    rotated = across_transform(gathered)
    back = lax.all_to_all(rotated, "tensor", 0, 0, axis_index_groups=same_core)
    sibling = jnp.dot(
        back[:, 1].reshape(chips * own, width), other_weight, preferred_element_type=jnp.float32
    )
    terms = product(back, sibling, down_weight)
    terms = lax.all_to_all(terms, "tensor", 0, 0, axis_index_groups=same_core)
    return jnp.sum(terms.astype(jnp.float32), axis=0).astype(jnp.bfloat16)


def solution(mesh):
    placed = (P("dp", "tensor"), P("dp", "tensor"), P("tensor"), P(), P("tensor", None))
    return jax.shard_map(
        per_device, mesh=mesh, in_specs=placed, out_specs=P(("dp", "tensor"), None), check_vma=False
    )
```

```python
import math

import jax
import jax.numpy as jnp
from jax import lax
from jax.experimental import pallas as pl
from jax.experimental.pallas import tpu as pltpu
from jax.sharding import PartitionSpec as P

FFN_UNITS = 28672
ORDER = 28
INNER = 32
SLAB = ORDER * INNER
LANES = 128
COLUMNS = 512
KEPT = 15


def outer_index(unit):
    return (unit * 2341) >> 16


def iota(shape, dim):
    return lax.broadcasted_iota(jnp.int32, shape, dim)


def picks(condition):
    return jnp.where(condition, 1.0, 0.0).astype(jnp.bfloat16)


def slab_matrix(hadamard):
    tall, wide = (SLAB, INNER), (INNER, SLAB)
    tall_unit, wide_unit = iota(tall, 0), iota(wide, 1)
    tall_outer, wide_outer = outer_index(tall_unit), outer_index(wide_unit)
    pick_outer = picks(wide_outer == iota(wide, 0))
    pick_inner = picks(wide_unit - ORDER * wide_outer == iota(wide, 0))[:ORDER]
    tall_inner = picks(tall_unit - ORDER * tall_outer == iota(tall, 1))[:, :ORDER]
    common = tall_outer & iota(tall, 1)
    for shift in (4, 2, 1):
        common = common ^ (common >> shift)
    outer_rows = (1 - 2 * (common & 1)).astype(jnp.float32).astype(jnp.bfloat16)
    inner_rows = jnp.dot(
        tall_inner,
        hadamard.astype(jnp.float32).astype(jnp.bfloat16),
        preferred_element_type=jnp.float32,
    ).astype(jnp.bfloat16)
    inner = jnp.dot(inner_rows, pick_inner, preferred_element_type=jnp.float32)
    outer = jnp.dot(outer_rows, pick_outer, preferred_element_type=jnp.float32)
    return (inner * outer).astype(jnp.bfloat16)


def local_kernel(
    gate_hbm, up_hbm, signs_hbm, hadamard_hbm, out, gate, up, signs, hadamard, matrix, arrived, ready
):
    width = gate.shape[1]
    small = [
        pltpu.make_async_copy(source, held, ready.at[index])
        for index, (source, held) in enumerate(((hadamard_hbm, hadamard), (signs_hbm, signs)))
    ]
    for copy in small:
        copy.start()
    copies = []
    for slab in range(width // SLAB):
        lanes = pl.ds(slab * SLAB, SLAB)
        pair = [
            pltpu.make_async_copy(source.at[:, lanes], held.at[:, lanes], arrived.at[slab, index])
            for index, (source, held) in enumerate(((gate_hbm, gate), (up_hbm, up)))
        ]
        for copy in pair:
            copy.start()
        copies.append(pair)
    for copy in small:
        copy.wait()
    matrix[...] = slab_matrix(hadamard[...])
    for slab, pair in enumerate(copies):
        for copy in pair:
            copy.wait()
        lanes = pl.ds(slab * SLAB, SLAB)
        half = 0.5 * gate[:, lanes].astype(jnp.float32)
        sign = signs[lanes].astype(jnp.float32).reshape(1, SLAB)
        hidden = (half + half * jnp.tanh(half)) * (up[:, lanes].astype(jnp.float32) * sign)
        out[:, lanes] = jnp.dot(
            hidden.astype(jnp.bfloat16), matrix[...], preferred_element_type=jnp.float32
        ).astype(jnp.bfloat16)


def local_transform(gate, up, signs, hadamard):
    tokens, width = gate.shape
    vmem = pl.BlockSpec(memory_space=pltpu.VMEM)
    return pl.pallas_call(
        local_kernel,
        in_specs=[pl.BlockSpec(memory_space=pl.ANY)] * 4,
        out_specs=vmem,
        out_shape=jax.ShapeDtypeStruct((tokens, width), jnp.bfloat16),
        scratch_shapes=[
            pltpu.VMEM((tokens, width), jnp.bfloat16),
            pltpu.VMEM((tokens, width), jnp.bfloat16),
            pltpu.VMEM((width,), jnp.int32),
            pltpu.VMEM((ORDER, ORDER), jnp.int32),
            pltpu.VMEM((SLAB, SLAB), jnp.bfloat16),
            pltpu.SemaphoreType.DMA((width // SLAB, 2)),
            pltpu.SemaphoreType.DMA((2,)),
        ],
        compiler_params=pltpu.CompilerParams(vmem_limit_bytes=59 << 20),
        name="local_transform",
    )(gate, up, signs, hadamard)


def across_kernel(source, out):
    devices, tokens, width = source.shape
    slabs = width // SLAB
    core = lax.axis_index("tensor") % 2
    for chunk in range(SLAB // LANES):
        values = []
        for device in range(devices):
            for slab in range(slabs):
                lanes = pl.ds(slab * SLAB + chunk * LANES, LANES)
                values.append(source[device, :, lanes].astype(jnp.float32))
        step = 1
        while step < len(values):
            for low in range(len(values)):
                if low & step == 0:
                    a, b = values[low], values[low | step]
                    values[low], values[low | step] = a + b, a - b
            step *= 2
        for index, value in enumerate(values):
            device, slab = divmod(index, slabs)
            chip, side = divmod(device, 2)
            lanes = pl.ds(slab * SLAB + chunk * LANES, LANES)
            place = core if side == 0 else 1 - core
            out[chip, place, :, lanes] = (value * (1.0 / math.sqrt(FFN_UNITS))).astype(jnp.bfloat16)


def across_transform(source):
    devices, tokens, width = source.shape
    return pl.pallas_call(
        across_kernel,
        in_specs=[pl.BlockSpec(memory_space=pltpu.VMEM)],
        out_specs=pl.BlockSpec(memory_space=pltpu.VMEM),
        out_shape=jax.ShapeDtypeStruct((devices // 2, 2, tokens, width), jnp.bfloat16),
        compiler_params=pltpu.CompilerParams(vmem_limit_bytes=20 << 20),
        name="across_transform",
    )(source)


def product_kernel(rows, other, own_hbm, out, own, spare, arrived):
    tiles = arrived.shape[0]
    chips, _, tokens, width = rows.shape
    kept = chips * KEPT
    lanes = lambda tile: pl.ds(pl.multiple_of(tile * COLUMNS, COLUMNS), COLUMNS)
    copy = lambda tile: pltpu.make_async_copy(
        own_hbm.at[:, lanes(tile)], own.at[:, lanes(tile)], arrived.at[tile]
    )
    for tile in range(tiles):
        copy(tile).start()
    square = (chips * tokens, chips * tokens)
    target = iota(square, 0)
    chip = (target * 4370) >> 16
    origin = jnp.where(
        target < kept, tokens * chip + target - KEPT * chip, tokens * (target - kept) + KEPT
    )
    order = picks(iota(square, 1) == origin)

    @pl.loop(0, tiles)
    def _(tile):
        copy(tile).wait()
        total = other[:, lanes(tile)] + jnp.dot(
            rows[:, 0].reshape(chips * tokens, width),
            own[:, lanes(tile)],
            preferred_element_type=jnp.float32,
        )
        ordered = jnp.dot(order, total.astype(jnp.bfloat16), preferred_element_type=jnp.float32)
        out[:, lanes(tile)] = ordered[:kept].astype(jnp.bfloat16)
        spare[pl.ds(pl.multiple_of(tile * chips, chips), chips), :] = ordered[kept:]

    shape = (kept, tiles * chips)
    piece, owner = iota(shape, 1) >> 3, iota(shape, 1) & 7
    place = picks(iota(shape, 0) == KEPT * owner + piece)
    out[:, tiles * COLUMNS :] = jnp.dot(
        place, spare[...].astype(jnp.bfloat16), preferred_element_type=jnp.float32
    ).astype(jnp.bfloat16)


def product(rows, other, own):
    chips, _, tokens, width = rows.shape
    columns = own.shape[1]
    tiles = columns // COLUMNS
    vmem = pl.BlockSpec(memory_space=pltpu.VMEM)
    return pl.pallas_call(
        product_kernel,
        in_specs=[vmem, vmem, pl.BlockSpec(memory_space=pl.ANY)],
        out_specs=vmem,
        out_shape=jax.ShapeDtypeStruct((chips * KEPT, columns + COLUMNS), jnp.bfloat16),
        scratch_shapes=[
            pltpu.VMEM(own.shape, own.dtype),
            pltpu.VMEM((tiles * chips, COLUMNS), jnp.float32),
            pltpu.SemaphoreType.DMA((tiles,)),
        ],
        compiler_params=pltpu.CompilerParams(vmem_limit_bytes=50 << 20),
        cost_estimate=pl.CostEstimate(
            flops=2 * chips * tokens * width * columns,
            transcendentals=0,
            bytes_accessed=own.size * own.dtype.itemsize,
        ),
        name="product",
    )(rows, other, own)


def unfold_kernel(source, out):
    columns = out.shape[1]
    shape = (out.shape[0], KEPT)
    straight = picks(iota(shape, 0) == iota(shape, 1))
    extra = source[:, columns:]
    for piece in range(columns // COLUMNS):
        lanes = pl.ds(piece * COLUMNS, COLUMNS)
        last = picks((iota(shape, 0) == KEPT) & (iota(shape, 1) == piece))
        out[:, lanes] = (
            jnp.dot(straight, source[:, lanes], preferred_element_type=jnp.float32)
            + jnp.dot(last, extra, preferred_element_type=jnp.float32)
        ).astype(jnp.bfloat16)


def unfold(source, tokens):
    vmem = pl.BlockSpec(memory_space=pltpu.VMEM)
    return pl.pallas_call(
        unfold_kernel,
        in_specs=[vmem],
        out_specs=vmem,
        out_shape=jax.ShapeDtypeStruct((tokens, source.shape[1] - COLUMNS), jnp.bfloat16),
        name="unfold",
    )(source)


def per_device(gate_pre, up_pre, signs, hadamard, down_weight):
    parts = lax.axis_size("tensor")
    tokens, width = gate_pre.shape
    own = tokens // parts
    chips = parts // 2
    same_core = [[2 * chip + side for chip in range(chips)] for side in range(2)]
    pairs = [(source, source ^ 1) for source in range(parts)]
    inner = local_transform(gate_pre, up_pre, signs, hadamard)
    inner, down_weight = lax.optimization_barrier((inner, down_weight))
    other_weight = lax.ppermute(down_weight, "tensor", pairs)
    gathered = lax.all_to_all(inner.reshape(parts, own, width), "tensor", 0, 0)
    rotated = across_transform(gathered)
    back = lax.all_to_all(rotated, "tensor", 0, 0, axis_index_groups=same_core)
    sibling = jnp.dot(
        back[:, 1].reshape(chips * own, width), other_weight, preferred_element_type=jnp.float32
    )
    terms = product(back, sibling, down_weight)
    total = lax.psum_scatter(
        terms, "tensor", scatter_dimension=0, axis_index_groups=same_core, tiled=True
    )
    return unfold(total, own)


def solution(mesh):
    placed = (P("dp", "tensor"), P("dp", "tensor"), P("tensor"), P(), P("tensor", None))
    return jax.shard_map(
        per_device, mesh=mesh, in_specs=placed, out_specs=P(("dp", "tensor"), None), check_vma=False
    )
```

```python
import math

import jax
import jax.numpy as jnp
from jax import lax
from jax.experimental import pallas as pl
from jax.experimental.pallas import tpu as pltpu
from jax.sharding import PartitionSpec as P

FFN_UNITS = 28672
ORDER = 28
INNER = 32
SLAB = ORDER * INNER
LANES = 128
COLUMNS = 512
TILE = 512
KEPT = 15


def outer_index(unit):
    return (unit * 2341) >> 16


def iota(shape, dim):
    return lax.broadcasted_iota(jnp.int32, shape, dim)


def picks(condition):
    return jnp.where(condition, 1.0, 0.0).astype(jnp.bfloat16)


def slab_matrix(hadamard):
    tall, wide = (SLAB, INNER), (INNER, SLAB)
    tall_unit, wide_unit = iota(tall, 0), iota(wide, 1)
    tall_outer, wide_outer = outer_index(tall_unit), outer_index(wide_unit)
    pick_outer = picks(wide_outer == iota(wide, 0))
    pick_inner = picks(wide_unit - ORDER * wide_outer == iota(wide, 0))[:ORDER]
    tall_inner = picks(tall_unit - ORDER * tall_outer == iota(tall, 1))[:, :ORDER]
    common = tall_outer & iota(tall, 1)
    for shift in (4, 2, 1):
        common = common ^ (common >> shift)
    outer_rows = (1 - 2 * (common & 1)).astype(jnp.float32).astype(jnp.bfloat16)
    inner_rows = jnp.dot(
        tall_inner,
        hadamard.astype(jnp.float32).astype(jnp.bfloat16),
        preferred_element_type=jnp.float32,
    ).astype(jnp.bfloat16)
    inner = jnp.dot(inner_rows, pick_inner, preferred_element_type=jnp.float32)
    outer = jnp.dot(outer_rows, pick_outer, preferred_element_type=jnp.float32)
    return (inner * outer).astype(jnp.bfloat16)


def local_kernel(
    gate_hbm, up_hbm, signs_hbm, hadamard_hbm, out, gate, up, signs, hadamard, matrix, arrived, ready
):
    width = gate.shape[1]
    small = [
        pltpu.make_async_copy(source, held, ready.at[index])
        for index, (source, held) in enumerate(((hadamard_hbm, hadamard), (signs_hbm, signs)))
    ]
    for copy in small:
        copy.start()
    copies = []
    for slab in range(width // SLAB):
        lanes = pl.ds(slab * SLAB, SLAB)
        pair = [
            pltpu.make_async_copy(source.at[:, lanes], held.at[:, lanes], arrived.at[slab, index])
            for index, (source, held) in enumerate(((gate_hbm, gate), (up_hbm, up)))
        ]
        for copy in pair:
            copy.start()
        copies.append(pair)
    for copy in small:
        copy.wait()
    matrix[...] = slab_matrix(hadamard[...])
    for slab, pair in enumerate(copies):
        for copy in pair:
            copy.wait()
        lanes = pl.ds(slab * SLAB, SLAB)
        half = 0.5 * gate[:, lanes].astype(jnp.float32)
        sign = signs[lanes].astype(jnp.float32).reshape(1, SLAB)
        hidden = (half + half * jnp.tanh(half)) * (up[:, lanes].astype(jnp.float32) * sign)
        out[:, lanes] = jnp.dot(
            hidden.astype(jnp.bfloat16), matrix[...], preferred_element_type=jnp.float32
        ).astype(jnp.bfloat16)


def local_transform(gate, up, signs, hadamard):
    tokens, width = gate.shape
    vmem = pl.BlockSpec(memory_space=pltpu.VMEM)
    return pl.pallas_call(
        local_kernel,
        in_specs=[pl.BlockSpec(memory_space=pl.ANY)] * 4,
        out_specs=vmem,
        out_shape=jax.ShapeDtypeStruct((tokens, width), jnp.bfloat16),
        scratch_shapes=[
            pltpu.VMEM((tokens, width), jnp.bfloat16),
            pltpu.VMEM((tokens, width), jnp.bfloat16),
            pltpu.VMEM((width,), jnp.int32),
            pltpu.VMEM((ORDER, ORDER), jnp.int32),
            pltpu.VMEM((SLAB, SLAB), jnp.bfloat16),
            pltpu.SemaphoreType.DMA((width // SLAB, 2)),
            pltpu.SemaphoreType.DMA((2,)),
        ],
        compiler_params=pltpu.CompilerParams(vmem_limit_bytes=20 << 20),
        name="local_transform",
    )(*(pltpu.with_memory_space_constraint(x, pltpu.HBM) for x in (gate, up, signs, hadamard)))


def across_kernel(source, out):
    devices, tokens, width = source.shape
    slabs = width // SLAB
    core = lax.axis_index("tensor") % 2
    for chunk in range(SLAB // LANES):
        values = []
        for device in range(devices):
            for slab in range(slabs):
                lanes = pl.ds(slab * SLAB + chunk * LANES, LANES)
                values.append(source[device, :, lanes].astype(jnp.float32))
        step = 1
        while step < len(values):
            for low in range(len(values)):
                if low & step == 0:
                    a, b = values[low], values[low | step]
                    values[low], values[low | step] = a + b, a - b
            step *= 2
        for index, value in enumerate(values):
            device, slab = divmod(index, slabs)
            chip, side = divmod(device, 2)
            lanes = pl.ds(slab * SLAB + chunk * LANES, LANES)
            place = core if side == 0 else 1 - core
            out[chip, place, :, lanes] = (value * (1.0 / math.sqrt(FFN_UNITS))).astype(jnp.bfloat16)


def across_transform(source):
    devices, tokens, width = source.shape
    return pl.pallas_call(
        across_kernel,
        in_specs=[pl.BlockSpec(memory_space=pltpu.VMEM)],
        out_specs=pl.BlockSpec(memory_space=pltpu.VMEM),
        out_shape=jax.ShapeDtypeStruct((devices // 2, 2, tokens, width), jnp.bfloat16),
        compiler_params=pltpu.CompilerParams(vmem_limit_bytes=20 << 20),
        name="across_transform",
    )(source)


def product_kernel(rows, other, own, out, ordered, spare):
    tiles = own.shape[1] // TILE
    chips, _, tokens, width = rows.shape
    kept = chips * KEPT
    columns = own.shape[1]
    lanes = lambda tile: pl.ds(pl.multiple_of(tile * TILE, TILE), TILE)
    square = (chips * tokens, chips * tokens)
    target = iota(square, 0)
    chip = (target * 4370) >> 16
    origin = jnp.where(
        target < kept, tokens * chip + target - KEPT * chip, tokens * (target - kept) + KEPT
    )
    order = picks(iota(square, 1) == origin)
    for place in (1, 0):
        ordered[place] = jnp.dot(
            order, rows[:, place].reshape(chips * tokens, width), preferred_element_type=jnp.float32
        ).astype(jnp.bfloat16)

    for tile in range(tiles):
        total = jnp.dot(ordered[1], other[:, lanes(tile)], preferred_element_type=jnp.float32)
        total += jnp.dot(ordered[0], own[:, lanes(tile)], preferred_element_type=jnp.float32)
        out[:, lanes(tile)] = total[:kept].astype(jnp.bfloat16)
        spare[:, lanes(tile)] = total[kept:].astype(jnp.bfloat16)

    shape = (kept, chips)
    row, owner = iota(shape, 0), iota(shape, 1)
    extra = jnp.zeros((kept, COLUMNS), jnp.float32)
    for piece in range(columns // COLUMNS):
        extra += jnp.dot(
            picks(row == KEPT * owner + piece),
            spare[:, pl.ds(piece * COLUMNS, COLUMNS)],
            preferred_element_type=jnp.float32,
        )
    out[:, columns:] = extra.astype(jnp.bfloat16)


def product(rows, other, own):
    chips, _, tokens, width = rows.shape
    columns = own.shape[1]
    vmem = pl.BlockSpec(memory_space=pltpu.VMEM)
    return pl.pallas_call(
        product_kernel,
        in_specs=[vmem, vmem, vmem],
        out_specs=vmem,
        out_shape=jax.ShapeDtypeStruct((chips * KEPT, columns + COLUMNS), jnp.bfloat16),
        scratch_shapes=[
            pltpu.VMEM((2, chips * tokens, width), jnp.bfloat16),
            pltpu.VMEM((chips, columns), jnp.bfloat16),
        ],
        compiler_params=pltpu.CompilerParams(vmem_limit_bytes=16 << 20),
        cost_estimate=pl.CostEstimate(
            flops=4 * chips * tokens * width * columns,
            transcendentals=0,
            bytes_accessed=own.size * own.dtype.itemsize,
        ),
        name="product",
    )(
        rows,
        pltpu.with_memory_space_constraint(other, pltpu.VMEM),
        pltpu.with_memory_space_constraint(own, pltpu.VMEM),
    )


def unfold_kernel(source, out):
    columns = out.shape[1]
    shape = (out.shape[0], KEPT)
    straight = picks(iota(shape, 0) == iota(shape, 1))
    extra = source[:, columns:]
    for piece in range(columns // COLUMNS):
        lanes = pl.ds(piece * COLUMNS, COLUMNS)
        last = picks((iota(shape, 0) == KEPT) & (iota(shape, 1) == piece))
        out[:, lanes] = (
            jnp.dot(straight, source[:, lanes], preferred_element_type=jnp.float32)
            + jnp.dot(last, extra, preferred_element_type=jnp.float32)
        ).astype(jnp.bfloat16)


def unfold(source, tokens):
    vmem = pl.BlockSpec(memory_space=pltpu.VMEM)
    return pl.pallas_call(
        unfold_kernel,
        in_specs=[vmem],
        out_specs=vmem,
        out_shape=jax.ShapeDtypeStruct((tokens, source.shape[1] - COLUMNS), jnp.bfloat16),
        name="unfold",
    )(source)


def per_device(gate_pre, up_pre, signs, hadamard, down_weight):
    parts = lax.axis_size("tensor")
    tokens, width = gate_pre.shape
    own = tokens // parts
    chips = parts // 2
    same_core = [[2 * chip + side for chip in range(chips)] for side in range(2)]
    pairs = [(source, source ^ 1) for source in range(parts)]
    inner = local_transform(gate_pre, up_pre, signs, hadamard)
    inner, down_weight = lax.optimization_barrier((inner, down_weight))
    other_weight = lax.ppermute(down_weight, "tensor", pairs)
    gathered = lax.all_to_all(inner.reshape(parts, own, width), "tensor", 0, 0)
    rotated = across_transform(gathered)
    rotated, other_weight = lax.optimization_barrier((rotated, other_weight))
    own_weight = lax.ppermute(other_weight, "tensor", pairs)
    back = lax.all_to_all(rotated, "tensor", 0, 0, axis_index_groups=same_core)
    terms = product(back, other_weight, own_weight)
    total = lax.psum_scatter(
        terms, "tensor", scatter_dimension=0, axis_index_groups=same_core, tiled=True
    )
    return unfold(total, own)


def solution(mesh):
    placed = (P("dp", "tensor"), P("dp", "tensor"), P("tensor"), P(), P("tensor", None))
    return jax.shard_map(
        per_device, mesh=mesh, in_specs=placed, out_specs=P(("dp", "tensor"), None), check_vma=False
    )
```

```python
import math

import jax
import jax.numpy as jnp
from jax import lax
from jax.experimental import pallas as pl
from jax.experimental.pallas import tpu as pltpu
from jax.sharding import PartitionSpec as P

FFN_UNITS = 28672
ORDER = 28
INNER = 32
SLAB = ORDER * INNER
LANES = 128
COLUMNS = 512
TILE = 512
KEPT = 15


def outer_index(unit):
    return (unit * 2341) >> 16


def iota(shape, dim):
    return lax.broadcasted_iota(jnp.int32, shape, dim)


def picks(condition):
    return jnp.where(condition, 1.0, 0.0).astype(jnp.bfloat16)


def slab_matrix(hadamard):
    tall, wide = (SLAB, INNER), (INNER, SLAB)
    tall_unit, wide_unit = iota(tall, 0), iota(wide, 1)
    tall_outer, wide_outer = outer_index(tall_unit), outer_index(wide_unit)
    pick_outer = picks(wide_outer == iota(wide, 0))
    pick_inner = picks(wide_unit - ORDER * wide_outer == iota(wide, 0))[:ORDER]
    tall_inner = picks(tall_unit - ORDER * tall_outer == iota(tall, 1))[:, :ORDER]
    common = tall_outer & iota(tall, 1)
    for shift in (4, 2, 1):
        common = common ^ (common >> shift)
    outer_rows = (1 - 2 * (common & 1)).astype(jnp.float32).astype(jnp.bfloat16)
    inner_rows = jnp.dot(
        tall_inner,
        hadamard.astype(jnp.float32).astype(jnp.bfloat16),
        preferred_element_type=jnp.float32,
    ).astype(jnp.bfloat16)
    inner = jnp.dot(inner_rows, pick_inner, preferred_element_type=jnp.float32)
    outer = jnp.dot(outer_rows, pick_outer, preferred_element_type=jnp.float32)
    return (inner * outer).astype(jnp.bfloat16)


def local_kernel(
    gate_hbm, up_hbm, signs_hbm, hadamard_hbm, out, gate, up, signs, hadamard, matrix, arrived, ready
):
    width = gate.shape[1]
    small = [
        pltpu.make_async_copy(source, held, ready.at[index])
        for index, (source, held) in enumerate(((hadamard_hbm, hadamard), (signs_hbm, signs)))
    ]
    for copy in small:
        copy.start()
    copies = []
    for slab in range(width // SLAB):
        lanes = pl.ds(slab * SLAB, SLAB)
        pair = [
            pltpu.make_async_copy(source.at[:, lanes], held.at[:, lanes], arrived.at[slab, index])
            for index, (source, held) in enumerate(((gate_hbm, gate), (up_hbm, up)))
        ]
        for copy in pair:
            copy.start()
        copies.append(pair)
    for copy in small:
        copy.wait()
    matrix[...] = slab_matrix(hadamard[...])
    for slab, pair in enumerate(copies):
        for copy in pair:
            copy.wait()
        lanes = pl.ds(slab * SLAB, SLAB)
        half = 0.5 * gate[:, lanes].astype(jnp.float32)
        sign = signs[lanes].astype(jnp.float32).reshape(1, SLAB)
        hidden = (half + half * jnp.tanh(half)) * (up[:, lanes].astype(jnp.float32) * sign)
        out[:, lanes] = jnp.dot(
            hidden.astype(jnp.bfloat16), matrix[...], preferred_element_type=jnp.float32
        ).astype(jnp.bfloat16)


def local_transform(gate, up, signs, hadamard):
    tokens, width = gate.shape
    vmem = pl.BlockSpec(memory_space=pltpu.VMEM)
    return pl.pallas_call(
        local_kernel,
        in_specs=[pl.BlockSpec(memory_space=pl.ANY)] * 4,
        out_specs=vmem,
        out_shape=jax.ShapeDtypeStruct((tokens, width), jnp.bfloat16),
        scratch_shapes=[
            pltpu.VMEM((tokens, width), jnp.bfloat16),
            pltpu.VMEM((tokens, width), jnp.bfloat16),
            pltpu.VMEM((width,), jnp.int32),
            pltpu.VMEM((ORDER, ORDER), jnp.int32),
            pltpu.VMEM((SLAB, SLAB), jnp.bfloat16),
            pltpu.SemaphoreType.DMA((width // SLAB, 2)),
            pltpu.SemaphoreType.DMA((2,)),
        ],
        compiler_params=pltpu.CompilerParams(vmem_limit_bytes=20 << 20),
        name="local_transform",
    )(*(pltpu.with_memory_space_constraint(x, pltpu.HBM) for x in (gate, up, signs, hadamard)))


def across_kernel(source, out):
    devices, tokens, width = source.shape
    slabs = width // SLAB
    core = lax.axis_index("tensor") % 2
    for chunk in range(SLAB // LANES):
        values = []
        for device in range(devices):
            for slab in range(slabs):
                lanes = pl.ds(slab * SLAB + chunk * LANES, LANES)
                values.append(source[device, :, lanes].astype(jnp.float32))
        step = 1
        while step < len(values):
            for low in range(len(values)):
                if low & step == 0:
                    a, b = values[low], values[low | step]
                    values[low], values[low | step] = a + b, a - b
            step *= 2
        for index, value in enumerate(values):
            device, slab = divmod(index, slabs)
            chip, side = divmod(device, 2)
            lanes = pl.ds(slab * SLAB + chunk * LANES, LANES)
            place = core if side == 0 else 1 - core
            out[chip, place, :, lanes] = (value * (1.0 / math.sqrt(FFN_UNITS))).astype(jnp.bfloat16)


def across_transform(source):
    devices, tokens, width = source.shape
    return pl.pallas_call(
        across_kernel,
        in_specs=[pl.BlockSpec(memory_space=pltpu.VMEM)],
        out_specs=pl.BlockSpec(memory_space=pltpu.VMEM),
        out_shape=jax.ShapeDtypeStruct((devices // 2, 2, tokens, width), jnp.bfloat16),
        compiler_params=pltpu.CompilerParams(vmem_limit_bytes=20 << 20),
        cost_estimate=pl.CostEstimate(flops=8_000_000_000, transcendentals=0, bytes_accessed=4_000_000),
        name="across_transform",
    )(source)


def product_kernel(rows, other, own, out, ordered, spare):
    tiles = own.shape[1] // TILE
    chips, _, tokens, width = rows.shape
    kept = chips * KEPT
    columns = own.shape[1]
    lanes = lambda tile: pl.ds(pl.multiple_of(tile * TILE, TILE), TILE)
    square = (chips * tokens, chips * tokens)
    target = iota(square, 0)
    chip = (target * 4370) >> 16
    origin = jnp.where(
        target < kept, tokens * chip + target - KEPT * chip, tokens * (target - kept) + KEPT
    )
    order = picks(iota(square, 1) == origin)
    for place in (1, 0):
        ordered[place] = jnp.dot(
            order, rows[:, place].reshape(chips * tokens, width), preferred_element_type=jnp.float32
        ).astype(jnp.bfloat16)

    for tile in range(tiles):
        total = jnp.dot(ordered[1], other[:, lanes(tile)], preferred_element_type=jnp.float32)
        total += jnp.dot(ordered[0], own[:, lanes(tile)], preferred_element_type=jnp.float32)
        out[:, lanes(tile)] = total[:kept].astype(jnp.bfloat16)
        spare[:, lanes(tile)] = total[kept:].astype(jnp.bfloat16)

    shape = (kept, chips)
    row, owner = iota(shape, 0), iota(shape, 1)
    extra = jnp.zeros((kept, COLUMNS), jnp.float32)
    for piece in range(columns // COLUMNS):
        extra += jnp.dot(
            picks(row == KEPT * owner + piece),
            spare[:, pl.ds(piece * COLUMNS, COLUMNS)],
            preferred_element_type=jnp.float32,
        )
    out[:, columns:] = extra.astype(jnp.bfloat16)


def product(rows, other, own):
    chips, _, tokens, width = rows.shape
    columns = own.shape[1]
    vmem = pl.BlockSpec(memory_space=pltpu.VMEM)
    return pl.pallas_call(
        product_kernel,
        in_specs=[vmem, vmem, vmem],
        out_specs=vmem,
        out_shape=jax.ShapeDtypeStruct((chips * KEPT, columns + COLUMNS), jnp.bfloat16),
        scratch_shapes=[
            pltpu.VMEM((2, chips * tokens, width), jnp.bfloat16),
            pltpu.VMEM((chips, columns), jnp.bfloat16),
        ],
        compiler_params=pltpu.CompilerParams(vmem_limit_bytes=16 << 20),
        cost_estimate=pl.CostEstimate(
            flops=4 * chips * tokens * width * columns,
            transcendentals=0,
            bytes_accessed=own.size * own.dtype.itemsize,
        ),
        name="product",
    )(
        rows,
        pltpu.with_memory_space_constraint(other, pltpu.VMEM),
        pltpu.with_memory_space_constraint(own, pltpu.VMEM),
    )


def unfold_kernel(source, out):
    columns = out.shape[1]
    out[:KEPT, :] = source[:, :columns]
    extra = source[:, columns:]
    for piece in range(columns // COLUMNS):
        out[KEPT:, pl.ds(piece * COLUMNS, COLUMNS)] = extra[piece : piece + 1]


def unfold(source, tokens):
    vmem = pl.BlockSpec(memory_space=pltpu.VMEM)
    return pl.pallas_call(
        unfold_kernel,
        in_specs=[vmem],
        out_specs=vmem,
        out_shape=jax.ShapeDtypeStruct((tokens, source.shape[1] - COLUMNS), jnp.bfloat16),
        name="unfold",
    )(source)


def per_device(gate_pre, up_pre, signs, hadamard, down_weight):
    parts = lax.axis_size("tensor")
    tokens, width = gate_pre.shape
    own = tokens // parts
    chips = parts // 2
    same_core = [[2 * chip + side for chip in range(chips)] for side in range(2)]
    pairs = [(source, source ^ 1) for source in range(parts)]
    inner = local_transform(gate_pre, up_pre, signs, hadamard)
    inner, down_weight = lax.optimization_barrier((inner, down_weight))
    other_weight = lax.ppermute(down_weight, "tensor", pairs)
    gathered = lax.all_to_all(inner.reshape(parts, own, width), "tensor", 0, 0)
    rotated = across_transform(gathered)
    back = lax.all_to_all(rotated, "tensor", 0, 0, axis_index_groups=same_core)
    terms = product(back, other_weight, down_weight)
    total = lax.psum_scatter(
        terms, "tensor", scatter_dimension=0, axis_index_groups=same_core, tiled=True
    )
    return unfold(total, own)


def solution(mesh):
    placed = (P("dp", "tensor"), P("dp", "tensor"), P("tensor"), P(), P("tensor", None))
    return jax.shard_map(
        per_device, mesh=mesh, in_specs=placed, out_specs=P(("dp", "tensor"), None), check_vma=False
    )
```

```python
import math

import jax
import jax.numpy as jnp
from jax import lax
from jax.experimental import pallas as pl
from jax.experimental.pallas import tpu as pltpu
from jax.sharding import PartitionSpec as P

FFN_UNITS = 28672
ORDER = 28
INNER = 32
SLAB = ORDER * INNER
LANES = 128
COLUMNS = 512
TILE = 512
KEPT = 15


def outer_index(unit):
    return (unit * 2341) >> 16


def iota(shape, dim):
    return lax.broadcasted_iota(jnp.int32, shape, dim)


def picks(condition):
    return jnp.where(condition, 1.0, 0.0).astype(jnp.bfloat16)


def outer_matrix():
    tall, wide = (SLAB, INNER), (INNER, SLAB)
    common = outer_index(iota(tall, 0)) & iota(tall, 1)
    for shift in (4, 2, 1):
        common = common ^ (common >> shift)
    rows = (1 - 2 * (common & 1)).astype(jnp.float32).astype(jnp.bfloat16)
    pick = picks(outer_index(iota(wide, 1)) == iota(wide, 0))
    return jnp.dot(rows, pick, preferred_element_type=jnp.float32).astype(jnp.bfloat16)


def inner_picks():
    tall, wide = iota((SLAB, ORDER), 0), iota((ORDER, SLAB), 1)
    return (
        picks(tall - ORDER * outer_index(tall) == iota((SLAB, ORDER), 1)),
        picks(wide - ORDER * outer_index(wide) == iota((ORDER, SLAB), 0)),
    )


def inner_matrix(hadamard, tall_pick, wide_pick):
    rows = jnp.dot(
        tall_pick,
        hadamard.astype(jnp.float32).astype(jnp.bfloat16),
        preferred_element_type=jnp.float32,
    )
    return jnp.dot(rows.astype(jnp.bfloat16), wide_pick, preferred_element_type=jnp.float32)


def local_kernel(
    gate_hbm, up_hbm, signs_hbm, hadamard_hbm, out, gate, up, signs, hadamard, matrix, arrived, ready
):
    width = gate.shape[1]
    small = [
        pltpu.make_async_copy(source, held, ready.at[index])
        for index, (source, held) in enumerate(((hadamard_hbm, hadamard), (signs_hbm, signs)))
    ]
    for copy in small:
        copy.start()
    copies = []
    for slab in range(width // SLAB):
        lanes = pl.ds(slab * SLAB, SLAB)
        pair = [
            pltpu.make_async_copy(source.at[:, lanes], held.at[:, lanes], arrived.at[slab, index])
            for index, (source, held) in enumerate(((gate_hbm, gate), (up_hbm, up)))
        ]
        for copy in pair:
            copy.start()
        copies.append(pair)
    matrix[...] = outer_matrix()
    tall_pick, wide_pick = inner_picks()
    for copy in small:
        copy.wait()
    inner = inner_matrix(hadamard[...], tall_pick, wide_pick)
    matrix[...] = inner.astype(jnp.bfloat16) * matrix[...]
    for pair in copies:
        for copy in pair:
            copy.wait()
    for slab in range(width // SLAB):
        lanes = pl.ds(slab * SLAB, SLAB)
        half = 0.5 * gate[:, lanes].astype(jnp.float32)
        sign = signs[lanes].astype(jnp.float32).reshape(1, SLAB)
        hidden = (half + half * jnp.tanh(half)) * (up[:, lanes].astype(jnp.float32) * sign)
        out[:, lanes] = jnp.dot(
            hidden.astype(jnp.bfloat16), matrix[...], preferred_element_type=jnp.float32
        ).astype(jnp.bfloat16)


def local_transform(gate, up, signs, hadamard):
    tokens, width = gate.shape
    vmem = pl.BlockSpec(memory_space=pltpu.VMEM)
    return pl.pallas_call(
        local_kernel,
        in_specs=[pl.BlockSpec(memory_space=pl.ANY)] * 4,
        out_specs=vmem,
        out_shape=jax.ShapeDtypeStruct((tokens, width), jnp.bfloat16),
        scratch_shapes=[
            pltpu.VMEM((tokens, width), jnp.bfloat16),
            pltpu.VMEM((tokens, width), jnp.bfloat16),
            pltpu.VMEM((width,), jnp.int32),
            pltpu.VMEM((ORDER, ORDER), jnp.int32),
            pltpu.VMEM((SLAB, SLAB), jnp.bfloat16),
            pltpu.SemaphoreType.DMA((width // SLAB, 2)),
            pltpu.SemaphoreType.DMA((2,)),
        ],
        compiler_params=pltpu.CompilerParams(vmem_limit_bytes=20 << 20),
        name="local_transform",
    )(*(pltpu.with_memory_space_constraint(x, pltpu.HBM) for x in (gate, up, signs, hadamard)))


def across_kernel(source, out):
    devices, tokens, width = source.shape
    slabs = width // SLAB
    core = lax.axis_index("tensor") % 2
    for chunk in range(SLAB // LANES):
        values = []
        for device in range(devices):
            for slab in range(slabs):
                lanes = pl.ds(slab * SLAB + chunk * LANES, LANES)
                values.append(source[device, :, lanes].astype(jnp.float32))
        step = 1
        while step < len(values):
            for low in range(len(values)):
                if low & step == 0:
                    a, b = values[low], values[low | step]
                    values[low], values[low | step] = a + b, a - b
            step *= 2
        for index, value in enumerate(values):
            device, slab = divmod(index, slabs)
            chip, side = divmod(device, 2)
            lanes = pl.ds(slab * SLAB + chunk * LANES, LANES)
            place = core if side == 0 else 1 - core
            out[chip, place, :, lanes] = (value * (1.0 / math.sqrt(FFN_UNITS))).astype(jnp.bfloat16)


def across_transform(source):
    devices, tokens, width = source.shape
    return pl.pallas_call(
        across_kernel,
        in_specs=[pl.BlockSpec(memory_space=pltpu.VMEM)],
        out_specs=pl.BlockSpec(memory_space=pltpu.VMEM),
        out_shape=jax.ShapeDtypeStruct((devices // 2, 2, tokens, width), jnp.bfloat16),
        compiler_params=pltpu.CompilerParams(vmem_limit_bytes=20 << 20),
        cost_estimate=pl.CostEstimate(
            flops=4_000_000_000, transcendentals=0, bytes_accessed=4_000_000
        ),
        name="across_transform",
    )(source)


def product_kernel(rows, other, own, out, ordered, spare):
    tiles = own.shape[1] // TILE
    chips, _, tokens, width = rows.shape
    kept = chips * KEPT
    columns = own.shape[1]
    lanes = lambda tile: pl.ds(pl.multiple_of(tile * TILE, TILE), TILE)
    square = (chips * tokens, chips * tokens)
    target = iota(square, 0)
    chip = (target * 4370) >> 16
    origin = jnp.where(
        target < kept, tokens * chip + target - KEPT * chip, tokens * (target - kept) + KEPT
    )
    order = picks(iota(square, 1) == origin)
    for place in (1, 0):
        ordered[place] = jnp.dot(
            order, rows[:, place].reshape(chips * tokens, width), preferred_element_type=jnp.float32
        ).astype(jnp.bfloat16)

    for tile in range(tiles):
        total = jnp.dot(ordered[1], other[:, lanes(tile)], preferred_element_type=jnp.float32)
        total += jnp.dot(ordered[0], own[:, lanes(tile)], preferred_element_type=jnp.float32)
        out[:, lanes(tile)] = total[:kept].astype(jnp.bfloat16)
        spare[:, lanes(tile)] = total[kept:].astype(jnp.bfloat16)

    shape = (kept, chips)
    row, owner = iota(shape, 0), iota(shape, 1)
    extra = jnp.zeros((kept, COLUMNS), jnp.float32)
    for piece in range(columns // COLUMNS):
        extra += jnp.dot(
            picks(row == KEPT * owner + piece),
            spare[:, pl.ds(piece * COLUMNS, COLUMNS)],
            preferred_element_type=jnp.float32,
        )
    out[:, columns:] = extra.astype(jnp.bfloat16)


def product(rows, other, own):
    chips, _, tokens, width = rows.shape
    columns = own.shape[1]
    vmem = pl.BlockSpec(memory_space=pltpu.VMEM)
    return pl.pallas_call(
        product_kernel,
        in_specs=[vmem, vmem, vmem],
        out_specs=vmem,
        out_shape=jax.ShapeDtypeStruct((chips * KEPT, columns + COLUMNS), jnp.bfloat16),
        scratch_shapes=[
            pltpu.VMEM((2, chips * tokens, width), jnp.bfloat16),
            pltpu.VMEM((chips, columns), jnp.bfloat16),
        ],
        compiler_params=pltpu.CompilerParams(vmem_limit_bytes=16 << 20),
        cost_estimate=pl.CostEstimate(
            flops=4 * chips * tokens * width * columns,
            transcendentals=0,
            bytes_accessed=own.size * own.dtype.itemsize,
        ),
        name="product",
    )(
        rows,
        pltpu.with_memory_space_constraint(other, pltpu.VMEM),
        pltpu.with_memory_space_constraint(own, pltpu.VMEM),
    )


def unfold_kernel(source, out):
    columns = out.shape[1]
    out[:KEPT, :] = source[:, :columns]
    extra = source[:, columns:]
    for piece in range(columns // COLUMNS):
        out[KEPT:, pl.ds(piece * COLUMNS, COLUMNS)] = extra[piece : piece + 1]


def unfold(source, tokens):
    vmem = pl.BlockSpec(memory_space=pltpu.VMEM)
    return pl.pallas_call(
        unfold_kernel,
        in_specs=[vmem],
        out_specs=vmem,
        out_shape=jax.ShapeDtypeStruct((tokens, source.shape[1] - COLUMNS), jnp.bfloat16),
        name="unfold",
    )(source)


def per_device(gate_pre, up_pre, signs, hadamard, down_weight):
    parts = lax.axis_size("tensor")
    tokens, width = gate_pre.shape
    own = tokens // parts
    chips = parts // 2
    same_core = [[2 * chip + side for chip in range(chips)] for side in range(2)]
    pairs = [(source, source ^ 1) for source in range(parts)]
    inner = local_transform(gate_pre, up_pre, signs, hadamard)
    inner, down_weight = lax.optimization_barrier((inner, down_weight))
    other_weight = lax.ppermute(down_weight, "tensor", pairs)
    gathered = lax.all_to_all(inner.reshape(parts, own, width), "tensor", 0, 0)
    rotated = across_transform(gathered)
    back = lax.all_to_all(rotated, "tensor", 0, 0, axis_index_groups=same_core)
    terms = product(back, other_weight, down_weight)
    total = lax.psum_scatter(
        terms, "tensor", scatter_dimension=0, axis_index_groups=same_core, tiled=True
    )
    return unfold(total, own)


def solution(mesh):
    placed = (P("dp", "tensor"), P("dp", "tensor"), P("tensor"), P(), P("tensor", None))
    return jax.shard_map(
        per_device, mesh=mesh, in_specs=placed, out_specs=P(("dp", "tensor"), None), check_vma=False
    )
```

```python
import math

import jax
import jax.numpy as jnp
from jax import lax
from jax.experimental import pallas as pl
from jax.experimental.pallas import tpu as pltpu
from jax.sharding import PartitionSpec as P

FFN_UNITS = 28672
ORDER = 28
INNER = 32
SLAB = ORDER * INNER
LANES = 128
COLUMNS = 512
TILE = 512
KEPT = 15


def outer_index(unit):
    return (unit * 2341) >> 16


def iota(shape, dim):
    return lax.broadcasted_iota(jnp.int32, shape, dim)


def picks(condition):
    return jnp.where(condition, 1.0, 0.0).astype(jnp.bfloat16)


def outer_matrix():
    tall, wide = (SLAB, INNER), (INNER, SLAB)
    common = outer_index(iota(tall, 0)) & iota(tall, 1)
    for shift in (4, 2, 1):
        common = common ^ (common >> shift)
    rows = (1 - 2 * (common & 1)).astype(jnp.float32).astype(jnp.bfloat16)
    pick = picks(outer_index(iota(wide, 1)) == iota(wide, 0))
    return jnp.dot(rows, pick, preferred_element_type=jnp.float32).astype(jnp.bfloat16)


def inner_picks():
    tall, wide = iota((SLAB, ORDER), 0), iota((ORDER, SLAB), 1)
    return (
        picks(tall - ORDER * outer_index(tall) == iota((SLAB, ORDER), 1)),
        picks(wide - ORDER * outer_index(wide) == iota((ORDER, SLAB), 0)),
    )


def inner_matrix(hadamard, tall_pick, wide_pick):
    rows = jnp.dot(
        tall_pick,
        hadamard.astype(jnp.float32).astype(jnp.bfloat16),
        preferred_element_type=jnp.float32,
    )
    return jnp.dot(rows.astype(jnp.bfloat16), wide_pick, preferred_element_type=jnp.float32)


def exchange_order(parts):
    return list(range(0, parts, 2)) + list(range(parts - 1, 0, -2))


def local_kernel(
    gate_hbm, up_hbm, signs_hbm, hadamard_hbm, out, gate, up, signs, hadamard, matrix, arrived, ready
):
    width = gate.shape[1]
    small = [
        pltpu.make_async_copy(source, held, ready.at[index])
        for index, (source, held) in enumerate(((hadamard_hbm, hadamard), (signs_hbm, signs)))
    ]
    for copy in small:
        copy.start()
    copies = []
    for slab in range(width // SLAB):
        lanes = pl.ds(slab * SLAB, SLAB)
        pair = [
            pltpu.make_async_copy(source.at[:, lanes], held.at[:, lanes], arrived.at[slab, index])
            for index, (source, held) in enumerate(((gate_hbm, gate), (up_hbm, up)))
        ]
        for copy in pair:
            copy.start()
        copies.append(pair)
    matrix[...] = outer_matrix()
    tall_pick, wide_pick = inner_picks()
    for copy in small:
        copy.wait()
    inner = inner_matrix(hadamard[...], tall_pick, wide_pick)
    matrix[...] = inner.astype(jnp.bfloat16) * matrix[...]
    for pair in copies:
        for copy in pair:
            copy.wait()
    for slab in range(width // SLAB):
        lanes = pl.ds(slab * SLAB, SLAB)
        half = 0.5 * gate[:, lanes].astype(jnp.float32)
        sign = signs[lanes].astype(jnp.float32).reshape(1, SLAB)
        hidden = (half + half * jnp.tanh(half)) * (up[:, lanes].astype(jnp.float32) * sign)
        result = jnp.dot(
            hidden.astype(jnp.bfloat16), matrix[...], preferred_element_type=jnp.float32
        ).astype(jnp.bfloat16)
        parts = lax.axis_size("tensor")
        own = gate.shape[0] // parts
        for position, device in enumerate(exchange_order(parts)):
            out[pl.ds(position * own, own), lanes] = result[device * own : (device + 1) * own]


def local_transform(gate, up, signs, hadamard):
    tokens, width = gate.shape
    vmem = pl.BlockSpec(memory_space=pltpu.VMEM)
    return pl.pallas_call(
        local_kernel,
        in_specs=[pl.BlockSpec(memory_space=pl.ANY)] * 4,
        out_specs=vmem,
        out_shape=jax.ShapeDtypeStruct((tokens, width), jnp.bfloat16),
        scratch_shapes=[
            pltpu.VMEM((tokens, width), jnp.bfloat16),
            pltpu.VMEM((tokens, width), jnp.bfloat16),
            pltpu.VMEM((width,), jnp.int32),
            pltpu.VMEM((ORDER, ORDER), jnp.int32),
            pltpu.VMEM((SLAB, SLAB), jnp.bfloat16),
            pltpu.SemaphoreType.DMA((width // SLAB, 2)),
            pltpu.SemaphoreType.DMA((2,)),
        ],
        compiler_params=pltpu.CompilerParams(vmem_limit_bytes=20 << 20),
        name="local_transform",
    )(*(pltpu.with_memory_space_constraint(x, pltpu.HBM) for x in (gate, up, signs, hadamard)))


def across_kernel(source, out):
    devices, tokens, width = source.shape
    slabs = width // SLAB
    core = lax.axis_index("tensor") % 2
    for chunk in range(SLAB // LANES):
        values = []
        for device in range(devices):
            position = exchange_order(devices).index(device)
            for slab in range(slabs):
                lanes = pl.ds(slab * SLAB + chunk * LANES, LANES)
                values.append(source[position, :, lanes].astype(jnp.float32))
        step = 1
        while step < len(values):
            for low in range(len(values)):
                if low & step == 0:
                    a, b = values[low], values[low | step]
                    values[low], values[low | step] = a + b, a - b
            step *= 2
        for index, value in enumerate(values):
            device, slab = divmod(index, slabs)
            chip, side = divmod(device, 2)
            lanes = pl.ds(slab * SLAB + chunk * LANES, LANES)
            place = core if side == 0 else 1 - core
            target = jnp.where(core == 0, chip, devices // 2 - 1 - chip)
            out[target, place, :, lanes] = (value * (1.0 / math.sqrt(FFN_UNITS))).astype(jnp.bfloat16)


def across_transform(source):
    devices, tokens, width = source.shape
    return pl.pallas_call(
        across_kernel,
        in_specs=[pl.BlockSpec(memory_space=pltpu.VMEM)],
        out_specs=pl.BlockSpec(memory_space=pltpu.VMEM),
        out_shape=jax.ShapeDtypeStruct((devices // 2, 2, tokens, width), jnp.bfloat16),
        compiler_params=pltpu.CompilerParams(vmem_limit_bytes=20 << 20),
        cost_estimate=pl.CostEstimate(
            flops=4_000_000_000, transcendentals=0, bytes_accessed=4_000_000
        ),
        name="across_transform",
    )(source)


def product_kernel(rows, other, own, out, ordered, spare):
    tiles = own.shape[1] // TILE
    chips, _, tokens, width = rows.shape
    kept = chips * KEPT
    columns = own.shape[1]
    lanes = lambda tile: pl.ds(pl.multiple_of(tile * TILE, TILE), TILE)
    square = (chips * tokens, chips * tokens)
    target = iota(square, 0)
    chip = (target * 4370) >> 16
    origin = jnp.where(
        target < kept, tokens * chip + target - KEPT * chip, tokens * (target - kept) + KEPT
    )
    order = picks(iota(square, 1) == origin)
    for place in (1, 0):
        ordered[place] = jnp.dot(
            order, rows[:, place].reshape(chips * tokens, width), preferred_element_type=jnp.float32
        ).astype(jnp.bfloat16)

    for tile in range(tiles):
        total = jnp.dot(ordered[1], other[:, lanes(tile)], preferred_element_type=jnp.float32)
        total += jnp.dot(ordered[0], own[:, lanes(tile)], preferred_element_type=jnp.float32)
        out[:, lanes(tile)] = total[:kept].astype(jnp.bfloat16)
        spare[:, lanes(tile)] = total[kept:].astype(jnp.bfloat16)

    shape = (kept, chips)
    row, owner = iota(shape, 0), iota(shape, 1)
    extra = jnp.zeros((kept, COLUMNS), jnp.float32)
    for piece in range(columns // COLUMNS):
        extra += jnp.dot(
            picks(row == KEPT * owner + piece),
            spare[:, pl.ds(piece * COLUMNS, COLUMNS)],
            preferred_element_type=jnp.float32,
        )
    out[:, columns:] = extra.astype(jnp.bfloat16)


def product(rows, other, own):
    chips, _, tokens, width = rows.shape
    columns = own.shape[1]
    vmem = pl.BlockSpec(memory_space=pltpu.VMEM)
    return pl.pallas_call(
        product_kernel,
        in_specs=[vmem, vmem, vmem],
        out_specs=vmem,
        out_shape=jax.ShapeDtypeStruct((chips * KEPT, columns + COLUMNS), jnp.bfloat16),
        scratch_shapes=[
            pltpu.VMEM((2, chips * tokens, width), jnp.bfloat16),
            pltpu.VMEM((chips, columns), jnp.bfloat16),
        ],
        compiler_params=pltpu.CompilerParams(vmem_limit_bytes=16 << 20),
        cost_estimate=pl.CostEstimate(
            flops=4 * chips * tokens * width * columns,
            transcendentals=0,
            bytes_accessed=own.size * own.dtype.itemsize,
        ),
        name="product",
    )(
        rows,
        pltpu.with_memory_space_constraint(other, pltpu.VMEM),
        pltpu.with_memory_space_constraint(own, pltpu.VMEM),
    )


def unfold_kernel(source, out):
    columns = out.shape[1]
    out[:KEPT, :] = source[:, :columns]
    extra = source[:, columns:]
    for piece in range(columns // COLUMNS):
        out[KEPT:, pl.ds(piece * COLUMNS, COLUMNS)] = extra[piece : piece + 1]


def unfold(source, tokens):
    vmem = pl.BlockSpec(memory_space=pltpu.VMEM)
    return pl.pallas_call(
        unfold_kernel,
        in_specs=[vmem],
        out_specs=vmem,
        out_shape=jax.ShapeDtypeStruct((tokens, source.shape[1] - COLUMNS), jnp.bfloat16),
        name="unfold",
    )(source)


def per_device(gate_pre, up_pre, signs, hadamard, down_weight):
    parts = lax.axis_size("tensor")
    tokens, width = gate_pre.shape
    own = tokens // parts
    chips = parts // 2
    pairs = [(source, source ^ 1) for source in range(parts)]
    inner = local_transform(gate_pre, up_pre, signs, hadamard)
    inner, down_weight = lax.optimization_barrier((inner, down_weight))
    other_weight = lax.ppermute(down_weight, "tensor", pairs)
    everyone = [exchange_order(parts)]
    same_core = [everyone[0][:chips], everyone[0][chips:]]
    gathered = lax.all_to_all(
        inner.reshape(parts, own, width), "tensor", 0, 0, axis_index_groups=everyone
    )
    rotated = across_transform(gathered)
    back = lax.all_to_all(rotated, "tensor", 0, 0, axis_index_groups=same_core)
    terms = product(back, other_weight, down_weight)
    total = lax.psum_scatter(
        terms, "tensor", scatter_dimension=0, axis_index_groups=same_core, tiled=True
    )
    return unfold(total, own)


def solution(mesh):
    placed = (P("dp", "tensor"), P("dp", "tensor"), P("tensor"), P(), P("tensor", None))
    return jax.shard_map(
        per_device, mesh=mesh, in_specs=placed, out_specs=P(("dp", "tensor"), None), check_vma=False
    )
```

```python
import math

import jax
import jax.numpy as jnp
from jax import lax
from jax.experimental import pallas as pl
from jax.experimental.pallas import tpu as pltpu
from jax.sharding import PartitionSpec as P

FFN_UNITS = 28672
ORDER = 28
INNER = 32
SLAB = ORDER * INNER
LANES = 128
COLUMNS = 512
TILE = 512
KEPT = 15


def outer_index(unit):
    return (unit * 2341) >> 16


def iota(shape, dim):
    return lax.broadcasted_iota(jnp.int32, shape, dim)


def picks(condition):
    return jnp.where(condition, 1.0, 0.0).astype(jnp.bfloat16)


def outer_matrix():
    tall, wide = (SLAB, INNER), (INNER, SLAB)
    common = outer_index(iota(tall, 0)) & iota(tall, 1)
    for shift in (4, 2, 1):
        common = common ^ (common >> shift)
    rows = (1 - 2 * (common & 1)).astype(jnp.float32).astype(jnp.bfloat16)
    pick = picks(outer_index(iota(wide, 1)) == iota(wide, 0))
    return jnp.dot(rows, pick, preferred_element_type=jnp.float32).astype(jnp.bfloat16)


def inner_picks():
    tall, wide = iota((SLAB, ORDER), 0), iota((ORDER, SLAB), 1)
    return (
        picks(tall - ORDER * outer_index(tall) == iota((SLAB, ORDER), 1)),
        picks(wide - ORDER * outer_index(wide) == iota((ORDER, SLAB), 0)),
    )


def inner_matrix(hadamard, tall_pick, wide_pick):
    rows = jnp.dot(
        tall_pick,
        hadamard.astype(jnp.float32).astype(jnp.bfloat16),
        preferred_element_type=jnp.float32,
    )
    return jnp.dot(rows.astype(jnp.bfloat16), wide_pick, preferred_element_type=jnp.float32)


def exchange_order(parts):
    return list(range(0, parts, 2)) + list(range(parts - 1, 0, -2))


def local_kernel(
    gate_hbm, up_hbm, signs_hbm, hadamard_hbm, out, gate, up, signs, hadamard, matrix, arrived, ready
):
    width = gate.shape[1]
    small = [
        pltpu.make_async_copy(source, held, ready.at[index])
        for index, (source, held) in enumerate(((hadamard_hbm, hadamard), (signs_hbm, signs)))
    ]
    for copy in small:
        copy.start()
    copies = []
    for slab in range(width // SLAB):
        lanes = pl.ds(slab * SLAB, SLAB)
        pair = [
            pltpu.make_async_copy(source.at[:, lanes], held.at[:, lanes], arrived.at[slab, index])
            for index, (source, held) in enumerate(((gate_hbm, gate), (up_hbm, up)))
        ]
        for copy in pair:
            copy.start()
        copies.append(pair)
    matrix[...] = outer_matrix()
    tall_pick, wide_pick = inner_picks()
    for copy in small:
        copy.wait()
    inner = inner_matrix(hadamard[...], tall_pick, wide_pick)
    matrix[...] = inner.astype(jnp.bfloat16) * matrix[...]
    for pair in copies:
        for copy in pair:
            copy.wait()
    for slab in range(width // SLAB):
        lanes = pl.ds(slab * SLAB, SLAB)
        half = 0.5 * gate[:, lanes].astype(jnp.float32)
        sign = signs[lanes].astype(jnp.float32).reshape(1, SLAB)
        hidden = (half + half * jnp.tanh(half)) * (up[:, lanes].astype(jnp.float32) * sign)
        result = jnp.dot(
            hidden.astype(jnp.bfloat16), matrix[...], preferred_element_type=jnp.float32
        ).astype(jnp.bfloat16)
        parts = lax.axis_size("tensor")
        own = gate.shape[0] // parts
        for position, device in enumerate(exchange_order(parts)):
            out[pl.ds(position * own, own), lanes] = result[device * own : (device + 1) * own]


def local_transform(gate, up, signs, hadamard):
    tokens, width = gate.shape
    vmem = pl.BlockSpec(memory_space=pltpu.VMEM)
    return pl.pallas_call(
        local_kernel,
        in_specs=[pl.BlockSpec(memory_space=pl.ANY)] * 4,
        out_specs=vmem,
        out_shape=jax.ShapeDtypeStruct((tokens, width), jnp.bfloat16),
        scratch_shapes=[
            pltpu.VMEM((tokens, width), jnp.bfloat16),
            pltpu.VMEM((tokens, width), jnp.bfloat16),
            pltpu.VMEM((width,), jnp.int32),
            pltpu.VMEM((ORDER, ORDER), jnp.int32),
            pltpu.VMEM((SLAB, SLAB), jnp.bfloat16),
            pltpu.SemaphoreType.DMA((width // SLAB, 2)),
            pltpu.SemaphoreType.DMA((2,)),
        ],
        compiler_params=pltpu.CompilerParams(vmem_limit_bytes=20 << 20),
        name="local_transform",
    )(*(pltpu.with_memory_space_constraint(x, pltpu.HBM) for x in (gate, up, signs, hadamard)))


def across_kernel(source, out):
    devices, tokens, width = source.shape
    slabs = width // SLAB
    core = lax.axis_index("tensor") % 2
    for chunk in range(SLAB // LANES):
        values = []
        for device in range(devices):
            position = exchange_order(devices).index(device)
            for slab in range(slabs):
                lanes = pl.ds(slab * SLAB + chunk * LANES, LANES)
                values.append(source[position, :, lanes].astype(jnp.float32))
        step = 1
        while step < len(values):
            for low in range(len(values)):
                if low & step == 0:
                    a, b = values[low], values[low | step]
                    values[low], values[low | step] = a + b, a - b
            step *= 2
        for index, value in enumerate(values):
            device, slab = divmod(index, slabs)
            chip, side = divmod(device, 2)
            lanes = pl.ds(slab * SLAB + chunk * LANES, LANES)
            place = core if side == 0 else 1 - core
            target = jnp.where(core == 0, chip, devices // 2 - 1 - chip)
            out[target, place, :, lanes] = (value * (1.0 / math.sqrt(FFN_UNITS))).astype(jnp.bfloat16)


def across_transform(source):
    devices, tokens, width = source.shape
    return pl.pallas_call(
        across_kernel,
        in_specs=[pl.BlockSpec(memory_space=pltpu.VMEM)],
        out_specs=pl.BlockSpec(memory_space=pltpu.VMEM),
        out_shape=jax.ShapeDtypeStruct((devices // 2, 2, tokens, width), jnp.bfloat16),
        compiler_params=pltpu.CompilerParams(vmem_limit_bytes=20 << 20),
        cost_estimate=pl.CostEstimate(
            flops=4_000_000_000, transcendentals=0, bytes_accessed=4_000_000
        ),
        name="across_transform",
    )(source)


def product_kernel(rows, other, own, out, ordered, spare):
    tiles = own.shape[1] // TILE
    chips, _, tokens, width = rows.shape
    kept = chips * KEPT
    columns = own.shape[1]
    lanes = lambda tile: pl.ds(pl.multiple_of(tile * TILE, TILE), TILE)
    square = (chips * tokens, chips * tokens)
    target = iota(square, 0)
    chip = (target * 4370) >> 16
    origin = jnp.where(
        target < kept, tokens * chip + target - KEPT * chip, tokens * (target - kept) + KEPT
    )
    order = picks(iota(square, 1) == origin)
    for place in (1, 0):
        ordered[place] = jnp.dot(
            order, rows[:, place].reshape(chips * tokens, width), preferred_element_type=jnp.float32
        ).astype(jnp.bfloat16)

    for tile in range(tiles):
        total = jnp.dot(ordered[1], other[:, lanes(tile)], preferred_element_type=jnp.float32)
        total += jnp.dot(ordered[0], own[:, lanes(tile)], preferred_element_type=jnp.float32)
        out[:, lanes(tile)] = total[:kept].astype(jnp.bfloat16)
        spare[:, lanes(tile)] = total[kept:].astype(jnp.bfloat16)

    shape = (kept, chips)
    row, owner = iota(shape, 0), iota(shape, 1)
    extra = jnp.zeros((kept, COLUMNS), jnp.float32)
    for piece in range(columns // COLUMNS):
        extra += jnp.dot(
            picks(row == KEPT * owner + piece),
            spare[:, pl.ds(piece * COLUMNS, COLUMNS)],
            preferred_element_type=jnp.float32,
        )
    out[:, columns:] = extra.astype(jnp.bfloat16)


def product(rows, other, own):
    chips, _, tokens, width = rows.shape
    columns = own.shape[1]
    vmem = pl.BlockSpec(memory_space=pltpu.VMEM)
    return pl.pallas_call(
        product_kernel,
        in_specs=[vmem, vmem, vmem],
        out_specs=vmem,
        out_shape=jax.ShapeDtypeStruct((chips * KEPT, columns + COLUMNS), jnp.bfloat16),
        scratch_shapes=[
            pltpu.VMEM((2, chips * tokens, width), jnp.bfloat16),
            pltpu.VMEM((chips, columns), jnp.bfloat16),
        ],
        compiler_params=pltpu.CompilerParams(vmem_limit_bytes=16 << 20),
        cost_estimate=pl.CostEstimate(
            flops=4 * chips * tokens * width * columns,
            transcendentals=0,
            bytes_accessed=own.size * own.dtype.itemsize,
        ),
        name="product",
    )(
        rows,
        pltpu.with_memory_space_constraint(other, pltpu.VMEM),
        pltpu.with_memory_space_constraint(own, pltpu.VMEM),
    )


def unfold_kernel(source, out):
    columns = out.shape[1]
    shape = (out.shape[0], KEPT)
    straight = picks(iota(shape, 0) == iota(shape, 1))
    extra = source[:, columns:]
    for piece in range(columns // COLUMNS):
        lanes = pl.ds(piece * COLUMNS, COLUMNS)
        last = picks((iota(shape, 0) == KEPT) & (iota(shape, 1) == piece))
        out[:, lanes] = (
            jnp.dot(straight, source[:, lanes], preferred_element_type=jnp.float32)
            + jnp.dot(last, extra, preferred_element_type=jnp.float32)
        ).astype(jnp.bfloat16)


def unfold(source, tokens):
    vmem = pl.BlockSpec(memory_space=pltpu.VMEM)
    return pl.pallas_call(
        unfold_kernel,
        in_specs=[vmem],
        out_specs=vmem,
        out_shape=jax.ShapeDtypeStruct((tokens, source.shape[1] - COLUMNS), jnp.bfloat16),
        name="unfold",
    )(source)


def per_device(gate_pre, up_pre, signs, hadamard, down_weight):
    parts = lax.axis_size("tensor")
    tokens, width = gate_pre.shape
    own = tokens // parts
    chips = parts // 2
    pairs = [(source, source ^ 1) for source in range(parts)]
    inner = local_transform(gate_pre, up_pre, signs, hadamard)
    inner, down_weight = lax.optimization_barrier((inner, down_weight))
    other_weight = lax.ppermute(down_weight, "tensor", pairs)
    everyone = [exchange_order(parts)]
    same_core = [everyone[0][:chips], everyone[0][chips:]]
    gathered = lax.all_to_all(
        inner.reshape(parts, own, width), "tensor", 0, 0, axis_index_groups=everyone
    )
    rotated = across_transform(gathered)
    back = lax.all_to_all(rotated, "tensor", 0, 0, axis_index_groups=same_core)
    terms = product(back, other_weight, down_weight)
    total = lax.psum_scatter(
        terms, "tensor", scatter_dimension=0, axis_index_groups=same_core, tiled=True
    )
    return unfold(total, own)


def solution(mesh):
    placed = (P("dp", "tensor"), P("dp", "tensor"), P("tensor"), P(), P("tensor", None))
    return jax.shard_map(
        per_device, mesh=mesh, in_specs=placed, out_specs=P(("dp", "tensor"), None), check_vma=False
    )
```
